256 devices in a mesh: segment: 4 (over y), row: 64 (over x, z, core).
Axes of the slice: x: 4, y: 4, z: 8, core: 2. Of those that a mesh axis runs over, the one named last changes fastest.
Arguments:
- latents: bfloat16 [4, 128, 128, 256], P(None, 'row'), may hold values from -6 to 6
- noise: bfloat16 [4, 4, 128, 128, 256], P('segment', None, 'row'), may hold values from -6 to 6
- timesteps: int32 [4, 4, 2], replicated, may hold values from 1 to 1000
- text: bfloat16 [4, 77, 4096], P('segment', None, 'row'), may hold values from -48 to 48
- text_weight: bfloat16 [4096, 256], P('row'), may hold values from -0.09375 to 0.09375
- time_weight: bfloat16 [256, 256], replicated, may hold values from -0.375 to 0.375
- film_weight: bfloat16 [4, 256, 512], P('segment'), may hold values from -0.375 to 0.375
- conv_weight: bfloat16 [4, 3, 3, 256, 256], P('segment'), may hold values from -0.125 to 0.125
- norm_gain: float32 [4, 256], P('segment'), may hold values from 0.5 to 1.5
Outputs:
- denoised: bfloat16 [4, 128, 128, 256], P('segment', 'row')
The draws below stay inside these ranges and needn't reach their ends.
All inputs are finite; a program needn't handle non-finite values.
Results may differ from the reference program's by a relative error of at most 0.012.
Values may be sent and summed in bfloat16 or wider, within the bound.
No kernel may reach another device: no remote copies, remote signals or barrier semaphores. Data moves between devices by JAX's collectives and lax.ppermute only.
A program may use at most 64 MiB of HBM per device.

```python
import jax
import jax.numpy as jnp
from jax import lax

C = 256
D_TEXT = 4096
TOK = 77
COLS = 128
STEPS = 2
SECTIONS = 4
MICRO = 4
HEIGHT = 128


def set_ends(values, stream_key, low, high):
    place = [jax.random.randint(jax.random.fold_in(stream_key, axis), (), 0, length) for axis, length in enumerate(values.shape)]
    main_axis = values.shape.index(max(values.shape))
    beside = place[:main_axis] + [(place[main_axis] + 1) % values.shape[main_axis]] + place[main_axis + 1:]
    return values.at[tuple(place)].set(low).at[tuple(beside)].set(high)


def block_scale(stream_key, dims, split, least, high):
    def one(axis_at, shards_of):
        draws = jax.random.uniform(jax.random.fold_in(jax.random.fold_in(stream_key, 6), axis_at), (shards_of,), jnp.float32, least / len(split), high / len(split))
        return jnp.repeat(jnp.exp(draws), dims[axis_at] // shards_of).reshape((-1,) + (1,) * (len(dims) - axis_at - 1))

    level = one(*split[0])
    for cut in split[1:]:
        level = level * one(*cut)
    return level


def bell_draw(stream_key, shape, spread, limit, cuts=(), held_as=jnp.bfloat16):
    factor_of = block_scale(stream_key, shape, cuts, -0.22, 0.18) if cuts else 1.0
    drawn = jax.random.normal(stream_key, shape, jnp.float32) * spread * factor_of
    return jnp.minimum(jnp.maximum(drawn, -limit), limit).astype(held_as)


def setup_inputs(seed: int = 0) -> dict:
    key_list = jax.random.split(jax.random.key(seed), 10)
    latents = bell_draw(key_list[0], (MICRO, HEIGHT, COLS, C), 1.0, 6.0, ((1, 64),))
    noise = bell_draw(key_list[1], (SECTIONS, MICRO, HEIGHT, COLS, C), 1.0, 6.0, ((0, 4), (2, 64)))
    timesteps = set_ends(jax.random.randint(key_list[2], (MICRO, SECTIONS, STEPS), 1, 1001), jax.random.fold_in(key_list[2], 1), 1, 1000).astype(jnp.int32)
    text = bell_draw(key_list[3], (MICRO, TOK, D_TEXT), 8.0, 48.0, ((0, 4), (2, 64)))
    text_weight = bell_draw(key_list[4], (D_TEXT, C), D_TEXT ** -0.5, 0.09375, ((0, 64),))
    time_weight = bell_draw(key_list[5], (C, C), C ** -0.5, 0.375)
    film_weight = bell_draw(key_list[6], (SECTIONS, C, 2 * C), C ** -0.5, 0.375, ((0, 4),))
    conv_weight = bell_draw(key_list[7], (SECTIONS, 3, 3, C, C), (9 * C) ** -0.5, 0.125, ((0, 4),))
    norm_gain = jnp.clip(1.0 + 0.1 * jax.random.normal(key_list[8], (SECTIONS, C), jnp.float32), 0.5, 1.5)
    return {"latents": latents, "noise": noise, "timesteps": timesteps, "text": text, "text_weight": text_weight, "time_weight": time_weight, "film_weight": film_weight, "conv_weight": conv_weight, "norm_gain": norm_gain}


def sinusoid(times, channels):
    half = channels // 2
    freqs = jnp.exp(-jnp.log(10000.0) * jnp.arange(half, dtype=jnp.float32) / half)
    angles = times.astype(jnp.float32)[..., None] * freqs
    return jnp.concatenate([jnp.cos(angles), jnp.sin(angles)], axis=-1).astype(jnp.bfloat16)

def conditioning(pooled, times, time_weight, film_matrix):
    channels = time_weight.shape[0]
    embed = sinusoid(times, channels)
    flat = embed.reshape(-1, channels)
    time_part = jax.nn.silu(jnp.dot(flat, time_weight, preferred_element_type=jnp.float32))
    time_part = time_part.reshape(times.shape + (channels,))
    cond = (pooled[:, None, :] + time_part).astype(jnp.bfloat16)
    film = jnp.dot(cond.reshape(-1, channels), film_matrix, preferred_element_type=jnp.float32)
    return film.reshape(times.shape + (2 * channels,))

def normalize(x, gain):
    values = x.astype(jnp.float32)
    scale_inv = lax.rsqrt(lax.optimization_barrier(jnp.mean(values * values, axis=-1, keepdims=True)) + 1e-06)
    return (values * scale_inv * gain).astype(jnp.bfloat16)

def convolve(padded, kernel):
    lead = padded.ndim - 2
    full = jnp.pad(padded, ((0, 0),) * (lead - 1) + ((0, 0), (1, 1), (0, 0)))
    rows = padded.shape[-3] - 2
    width = padded.shape[-2]
    channels = padded.shape[-1]
    out_shape = padded.shape[:-3] + (rows, width, channels)
    total = None
    for dy in range(3):
        for dx in range(3):
            piece = full[..., dy:dy + rows, dx:dx + width, :].reshape(-1, channels)
            term = jnp.dot(piece, kernel[dy, dx], preferred_element_type=jnp.float32)
            total = term if total is None else total + term
    return total.reshape(out_shape)

def advance(x, padded, kernel, film, extra):
    channels = x.shape[-1]
    conv = convolve(padded, kernel)
    branch = jax.nn.silu(conv * (1.0 + film[..., :channels]) + film[..., channels:])
    return (x.astype(jnp.float32) + branch + extra).astype(jnp.bfloat16)

def reference(latents, noise, timesteps, text, text_weight, time_weight, film_weight, conv_weight, norm_gain):
    text_mean = lax.optimization_barrier(jnp.mean(text.astype(jnp.float32), axis=1)).astype(jnp.bfloat16)
    pooled = jnp.dot(text_mean, text_weight, preferred_element_type=jnp.float32)
    x = latents
    for section in range(SECTIONS):
        film = conditioning(pooled, timesteps[:, section], time_weight, film_weight[section])
        sigma = timesteps[:, section, STEPS - 1].astype(jnp.float32) / 1000.0
        for step in range(STEPS):
            normed = normalize(x, norm_gain[section])
            padded = jnp.pad(normed, ((0, 0), (1, 1), (0, 0), (0, 0)))
            extra = 0.0
            if step == STEPS - 1:
                extra = sigma[:, None, None, None] * noise[section].astype(jnp.float32)
            x = advance(x, padded, conv_weight[section], film[:, step][:, None, None, :], extra)
    return x
```

```python
import functools

import jax
import jax.numpy as jnp
from jax import lax
from jax.experimental import pallas as pl
from jax.experimental.pallas import tpu as pltpu
from jax.sharding import PartitionSpec as P

STEPS = 2
GAIN_ROWS = 16


def sinusoid(times, channels):
    half = channels // 2
    freqs = jnp.exp(-jnp.log(10000.0) * jnp.arange(half, dtype=jnp.float32) / half)
    angles = times.astype(jnp.float32)[..., None] * freqs
    return jnp.concatenate([jnp.cos(angles), jnp.sin(angles)], axis=-1).astype(jnp.bfloat16)


def pool_kernel(text_ref, weight_ref, out_ref):
    tokens = text_ref.shape[1]
    total = jnp.sum(text_ref[0].astype(jnp.float32), axis=0, keepdims=True)
    mean = (total / tokens).astype(jnp.bfloat16)
    part = jnp.dot(mean, weight_ref[...], preferred_element_type=jnp.float32)
    out_ref[...] = jnp.broadcast_to(part[None], out_ref.shape)


def section_kernel(
    section,
    height,
    ints_ref,
    sigma_ref,
    x_ref,
    across_ref,
    beyond_ref,
    parts_ref,
    tpart_ref,
    conv_ref,
    film_ref,
    pay_ref,
    got1_ref,
    got2_ref,
    got3_ref,
    swap1_ref,
    swap2_ref,
    swap3_ref,
    noise_ref,
    noise1_ref,
    noise2_ref,
    noise3_ref,
    out_ref,
    conv_buf,
    film_buf,
    gain_buf,
    noise_buf,
    xs,
    lhs,
    mid,
    sems,
):
    behind = ints_ref[0]
    core = ints_ref[1]
    first = ints_ref[2]
    micro = ints_ref[3]
    rows, cols, channels = xs.shape
    taps = conv_buf.shape[0]
    half = taps // 2

    def copies(j):
        if j == 0:
            pairs = [
                (conv_ref, conv_buf),
                (film_ref.at[:, :channels], film_buf.at[0]),
                (film_ref.at[:, channels:], film_buf.at[1]),
                (pay_ref.at[pl.ds(half + channels, GAIN_ROWS)], gain_buf),
                (noise_ref.at[micro], noise_buf),
            ]
        else:
            got = (got1_ref, got2_ref, got3_ref)[j - 1]
            swap = (swap1_ref, swap2_ref, swap3_ref)[j - 1]
            noise = (noise1_ref, noise2_ref, noise3_ref)[j - 1]
            here = pl.ds(pl.multiple_of(core * half, half), half)
            there = pl.ds(pl.multiple_of((1 - core) * half, half), half)
            pairs = [
                (got.at[pl.ds(0, half)], conv_buf.at[here]),
                (swap.at[pl.ds(0, half)], conv_buf.at[there]),
                (got.at[pl.ds(half, channels)], film_buf.at[core]),
                (swap.at[pl.ds(half, channels)], film_buf.at[1 - core]),
                (got.at[pl.ds(half + channels, GAIN_ROWS)], gain_buf),
                (noise, noise_buf),
            ]
        return [pltpu.make_async_copy(a, b, sems.at[i]) for i, (a, b) in enumerate(pairs)]

    for j in range(4):

        @pl.when(behind == j)
        def _(j=j):
            for copy in copies(j):
                copy.start()

    xs[2:4] = x_ref[...]
    xs[pl.ds(4 * (1 - core), 2)] = across_ref[...]
    xs[pl.ds(4 * core, 2)] = beyond_ref[...]

    for j in range(4):

        @pl.when(behind == j)
        def _(j=j):
            for copy in copies(j):
                copy.wait()

    gains = gain_buf[...].astype(jnp.float32)
    gain = gains[0:1] + gains[1:2] + gains[2:3]
    pooled = jnp.sum(parts_ref[...], axis=0)
    cond = (pooled + tpart_ref[...]).astype(jnp.bfloat16)
    scales = 1.0 + jnp.dot(cond, film_buf[0], preferred_element_type=jnp.float32)
    shifts = jnp.dot(cond, film_buf[1], preferred_element_type=jnp.float32)
    place = lax.broadcasted_iota(jnp.int32, (cols, channels), 0)

    for step in range(STEPS):
        source = xs if step == 0 else mid
        count = rows - 2 * step
        for i in range(count):
            values = source[i].astype(jnp.float32)
            inv = lax.rsqrt(jnp.mean(values * values, axis=-1, keepdims=True) + 1e-06)
            normed = values * inv * gain
            if step > 0:
                image_row = first + i + step
                inside = (image_row >= 0) & (image_row < height)
                normed = jnp.where(inside, normed, 0.0)
            at = pl.ds(i * cols, cols)
            left = jnp.where(place == 0, 0.0, pltpu.roll(normed, 1, 0))
            right = jnp.where(place == cols - 1, 0.0, pltpu.roll(normed, cols - 1, 0))
            lhs[at, 0:channels] = left.astype(jnp.bfloat16)
            lhs[at, channels : 2 * channels] = normed.astype(jnp.bfloat16)
            lhs[at, 2 * channels :] = right.astype(jnp.bfloat16)
        scale = scales[step : step + 1]
        shift = shifts[step : step + 1]
        for i in range(0, count - 2, 2):
            total = None
            for dy in range(3):
                term = jnp.dot(
                    lhs[pl.ds((i + dy) * cols, 2 * cols), :],
                    conv_buf[pl.ds(dy * 3 * channels, 3 * channels), :],
                    preferred_element_type=jnp.float32,
                )
                total = term if total is None else total + term
            moved = total * scale + shift
            branch = moved * (0.5 + 0.5 * jnp.tanh(0.5 * moved))
            before = source[i + 1 : i + 3].astype(jnp.float32).reshape(2 * cols, channels)
            after = before + branch
            if step == STEPS - 1:
                fresh = noise_buf[i : i + 2].astype(jnp.float32).reshape(2 * cols, channels)
                after = after + sigma_ref[section] * fresh
            after = after.astype(jnp.bfloat16).reshape(2, cols, channels)
            if step == STEPS - 1:
                out_ref[i : i + 2] = after
            else:
                mid[i : i + 2] = after


def body(
    latents, noise, timesteps, text, text_weight, time_weight, film_weight, conv_weight, norm_gain
):
    sections = lax.axis_size("segment")
    count = lax.axis_size("row")
    segment = lax.axis_index("segment")
    row = lax.axis_index("row")
    core = row % 2
    own, cols, channels = latents.shape[1:]
    height = own * count
    taps = 9 * channels
    half = taps // 2

    vmem = pl.BlockSpec(memory_space=pltpu.VMEM)
    smem = pl.BlockSpec(memory_space=pltpu.SMEM)
    hbm = pl.BlockSpec(memory_space=pl.ANY)

    conv = conv_weight.reshape(taps, channels)
    film = film_weight[0]
    top = norm_gain.astype(jnp.bfloat16)
    rest = norm_gain - top.astype(jnp.float32)
    middle = rest.astype(jnp.bfloat16)
    low = (rest - middle.astype(jnp.float32)).astype(jnp.bfloat16)
    gains = jnp.concatenate([top, middle, low, jnp.zeros((GAIN_ROWS - 3, channels), jnp.bfloat16)])
    payload = jnp.concatenate(
        [
            lax.dynamic_slice_in_dim(conv, core * half, half, 0),
            lax.dynamic_slice_in_dim(film, core * channels, channels, 1),
            gains,
        ]
    )
    swap_cores = [(i, i ^ 1) for i in range(count)]
    swap_chips = [(i, i + 1) for i in range(1, count - 1, 2)]
    swap_chips = swap_chips + [(b, a) for a, b in swap_chips]

    def turned(value, k):
        return lax.ppermute(value, "segment", [(i, (i + k) % sections) for i in range(sections)])

    got = {k: turned(payload, k) for k in (1, 3, 2)}

    parts = pl.pallas_call(
        pool_kernel,
        out_shape=jax.ShapeDtypeStruct((count, 1, channels), jnp.float32),
        in_specs=[vmem, vmem],
        out_specs=vmem,
    )(text, text_weight)
    parts = lax.all_to_all(parts, "row", split_axis=0, concat_axis=0, tiled=True)

    my_times = lax.dynamic_index_in_dim(timesteps, segment, 0, keepdims=False)
    embed = sinusoid(my_times, channels).reshape(-1, channels)
    tpart = jax.nn.silu(jnp.dot(embed, time_weight, preferred_element_type=jnp.float32))
    tpart = tpart.reshape(sections, STEPS, channels)
    sigma = my_times[:, STEPS - 1].astype(jnp.float32) / 1000.0

    fresh = {}
    for k in (1, 3, 2):
        mine = lax.dynamic_index_in_dim(noise[0], (segment + k) % sections, 0, keepdims=False)
        fresh[k] = turned(mine, k)
    swapped = {k: lax.ppermute(got[k], "row", swap_cores) for k in (1, 3, 2)}

    x = lax.dynamic_index_in_dim(latents, segment, 0, keepdims=False)
    for section in range(sections):
        across = lax.ppermute(x, "row", swap_cores)
        beyond = lax.ppermute(x, "row", swap_chips)
        ints = jnp.stack(
            [(segment - section) % sections, core, row * own - 2, segment]
        ).astype(jnp.int32)
        x = pl.pallas_call(
            functools.partial(section_kernel, section, height),
            out_shape=jax.ShapeDtypeStruct((own, cols, channels), jnp.bfloat16),
            in_specs=[smem, smem] + [vmem] * 5 + [hbm] * 13,
            out_specs=vmem,
            scratch_shapes=[
                pltpu.VMEM((taps, channels), jnp.bfloat16),
                pltpu.VMEM((2, channels, channels), jnp.bfloat16),
                pltpu.VMEM((GAIN_ROWS, channels), jnp.bfloat16),
                pltpu.VMEM((own, cols, channels), jnp.bfloat16),
                pltpu.VMEM((own + 4, cols, channels), jnp.bfloat16),
                pltpu.VMEM(((own + 4) * cols, 3 * channels), jnp.bfloat16),
                pltpu.VMEM((own + 2, cols, channels), jnp.bfloat16),
                pltpu.SemaphoreType.DMA((6,)),
            ],
            compiler_params=pltpu.CompilerParams(vmem_limit_bytes=32 * 1024 * 1024),
        )(
            ints,
            sigma,
            x,
            across,
            beyond,
            parts,
            tpart[section],
            conv,
            film,
            payload,
            got[1],
            got[2],
            got[3],
            swapped[1],
            swapped[2],
            swapped[3],
            noise[0],
            fresh[1],
            fresh[2],
            fresh[3],
        )
    return x[None]


def solution(mesh):
    in_specs = (
        P(None, "row", None, None),
        P("segment", None, "row", None, None),
        P(),
        P("segment", None, "row"),
        P("row", None),
        P(),
        P("segment", None, None),
        P("segment", None, None, None, None),
        P("segment", None),
    )
    out_specs = P("segment", "row", None, None)
    return jax.shard_map(body, mesh=mesh, in_specs=in_specs, out_specs=out_specs, check_vma=False)
```

```python
import functools
import math

import jax
import jax.numpy as jnp
from jax import lax
from jax.experimental import pallas as pl
from jax.experimental.pallas import tpu as pltpu
from jax.sharding import PartitionSpec as P

STEPS = 2
GAIN_ROWS = 16
MIB = 1024 * 1024


def place_of_device():
    row = lax.axis_index("row")
    return lax.axis_index("segment"), row, lax.rem(row, 2)


def prepare_kernel(
    latents, noise, conv, film, gain, x_out, pay0, pay1, more0, more1, noise2, sems
):
    segment, _, core = place_of_device()
    half = conv.shape[0] // 2
    channels = conv.shape[1]
    cols = latents.shape[2]
    cut = pay0.shape[0]
    start = core * half
    before, after = (noise.at[lax.rem(segment + k, 4)] for k in (3, 1))
    pairs = [(latents.at[segment], x_out), (noise.at[lax.rem(segment + 2, 4)], noise2)]
    for target in (pay0, more0):
        pairs.append((conv.at[pl.ds(pl.multiple_of(start, 16), cut)], target.at[pl.ds(0, cut)]))
    for target in (pay1, more1):
        source = conv.at[pl.ds(pl.multiple_of(start + cut, 16), half - cut)]
        pairs.append((source, target.at[pl.ds(0, half - cut)]))
    for i in range(2):
        pairs.append((before.at[i], more0.at[pl.ds(cut + i * cols, cols)]))
        pairs.append((after.at[i], more1.at[pl.ds(pay1.shape[0] + i * cols, cols)]))
    copies = [pltpu.make_async_copy(a, b, sems.at[i]) for i, (a, b) in enumerate(pairs)]
    film_at = pl.ds(half - cut, channels)
    sides = [
        [
            pltpu.make_async_copy(
                film.at[:, i * channels : (i + 1) * channels], target.at[film_at], sems.at[10 + j]
            )
            for j, target in enumerate((pay1, more1))
        ]
        for i in range(2)
    ]
    for copy in copies:
        copy.start()
    for i in range(2):

        @pl.when(core == i)
        def _(i=i):
            for copy in sides[i]:
                copy.start()

    exact = gain[...]
    top = exact.astype(jnp.bfloat16).astype(jnp.float32)
    middle = (exact - top).astype(jnp.bfloat16).astype(jnp.float32)
    low = exact - top - middle
    line = lax.broadcasted_iota(jnp.int32, (GAIN_ROWS, channels), 0)
    rows = jnp.where(line == 0, top, jnp.where(line == 1, middle, jnp.where(line == 2, low, 0.0)))
    for target in (pay1, more1):
        target[pl.ds(half - cut + channels, GAIN_ROWS), :] = rows.astype(jnp.bfloat16)
    for copy in copies:
        copy.wait()
    for i in range(2):

        @pl.when(core == i)
        def _(i=i):
            for copy in sides[i]:
                copy.wait()


def condition_kernel(times, text, text_weight, time_weight, x_core, parts_out, tpart_out):
    segment, _, _ = place_of_device()
    tokens = text.shape[1]
    channels = time_weight.shape[0]
    total = jnp.sum(text[0].astype(jnp.float32), axis=0, keepdims=True)
    mean = (total / tokens).astype(jnp.bfloat16)
    part = jnp.dot(mean, text_weight[...], preferred_element_type=jnp.float32)
    parts_out[...] = jnp.broadcast_to(part[None], parts_out.shape)
    count = tpart_out.shape[0]
    half = channels // 2
    line = lax.broadcasted_iota(jnp.int32, (count, half), 0)
    moments = jnp.zeros((count, half), jnp.float32)
    for i in range(count):
        now = times[segment, i // STEPS, i % STEPS].astype(jnp.float32)
        moments = jnp.where(line == i, now, moments)
    place = lax.broadcasted_iota(jnp.int32, (count, half), 1).astype(jnp.float32)
    angles = moments * jnp.exp(-math.log(10000.0) * place / half)
    embed = jnp.concatenate([jnp.cos(angles), jnp.sin(angles)], axis=-1).astype(jnp.bfloat16)
    value = jnp.dot(embed, time_weight[...], preferred_element_type=jnp.float32)
    tpart_out[...] = value * (0.5 + 0.5 * jnp.tanh(0.5 * value))


def after_kernel(first, second, parts, first_out, second_out):
    pass


def choose_kernel(noise, more1, noise2, more0, first, n_out, sems):
    segment, _, _ = place_of_device()
    sections = 4
    cols = n_out.shape[1]
    for act in ("start", "wait"):
        for section in range(sections - 1):
            behind = lax.rem(segment - section + sections, sections)
            for j in range(sections):

                @pl.when(behind == j)
                def _(j=j, section=section):
                    for i in range(2):
                        source = noise_row(j, i, cols, noise.at[segment], more1, noise2, more0)
                        target = n_out.at[2 * section + i]
                        copy = pltpu.make_async_copy(source, target, sems.at[section, i])
                        getattr(copy, act)()


def noise_row(j, i, cols, own, more1, noise2, more0):
    if j in (0, 2):
        return (own if j == 0 else noise2).at[i]
    source = more1 if j == 1 else more0
    return source.at[pl.ds(source.shape[0] - (2 - i) * cols, cols)]


def cascade_kernel(sections, height, names, *refs):
    r = dict(zip(names, refs))
    segment, row, core = place_of_device()
    lhs, mid, xs = r["lhs"], r["mid"], r["xs"]
    taps, channels = r["conv"].shape
    cols = xs.shape[1]
    half = taps // 2
    own = 2
    total_sections = r["tpart"].shape[0] // STEPS
    leading = sections[0] == 0

    strips = {}
    if leading:
        near, far, back = (r["near"], r["far"], r["back"])
        strips["xs"] = [
            (r["latents"].at[segment], 8, 8),
            (r["x_core"], 10, 6),
            (near.at[0:2], 4, 12),
            (near.at[2:4], 6, 10),
            (far.at[0:2], 0, 16),
            (far.at[2:4], 2, 14),
            (back.at[0:2], 14, 2),
            (back.at[2:4], 12, 4),
            (back.at[4:6], 16, 0),
        ]
    else:
        (n, n_core, n_near, n_far, n_back) = (
            r[key] for key in ("n", "n_core", "n_near", "n_far", "n_back")
        )
        strips["noise0"] = [
            (n.at[0:2], 6, 6),
            (n_core.at[0:2], 8, 4),
            (n_near.at[0:2], 2, 10),
            (n_near.at[4:6], 4, 8),
            (n_far, 0, 12),
            (n_back.at[0:2], 12, 0),
            (n_back.at[2:4], 10, 2),
        ]
        strips["noise1"] = [
            (n.at[2:4], 4, 4),
            (n_core.at[2:4], 6, 2),
            (n_near.at[2:4], 0, 8),
            (n_near.at[6:8], 2, 6),
            (n_back.at[4:6], 8, 0),
        ]
        strips["noise2"] = [(n.at[4:6], 2, 2), (n_core.at[4:6], 4, 0), (n_near.at[8:10], 0, 4)]
    moves = {}
    for key, placed in strips.items():
        moves[key] = []
        for i, (value, first, second) in enumerate(placed):
            target = r[key].at[pl.ds(first + core * (second - first), 2)]
            moves[key].append(pltpu.make_async_copy(value, target, r["strip_sems"].at[len(moves), i]))

    def weights_of(section):
        slot = section - sections[0]
        return [r[key].at[slot] for key in ("conv_buf", "film_buf", "gain_buf")]

    def copies(section, j, which):
        weights, films, gains = weights_of(section)
        sems = r["sems"].at[section]
        if j == 0:
            small = [
                (r["film"].at[:, :channels], films.at[0]),
                (r["film"].at[:, channels:], films.at[1]),
            ]
            large = [(r["conv"], weights)]
        else:
            cut = r["got1_0"].shape[0]
            small, large = ([], [])
            for key, side in (("got", core), ("swap", 1 - core)):
                part0, part1 = (r["%s%d_%d" % (key, j, i)] for i in range(2))
                if not small:
                    small.append((part1.at[pl.ds(half - cut + channels, GAIN_ROWS)], gains))
                at0 = pl.multiple_of(side * half, 16)
                at1 = pl.multiple_of(side * half + cut, 16)
                large.append((part0.at[pl.ds(0, cut)], weights.at[pl.ds(at0, cut)]))
                large.append((part1.at[pl.ds(0, half - cut)], weights.at[pl.ds(at1, half - cut)]))
                small.append((part1.at[pl.ds(half - cut, channels)], films.at[side]))
        pairs = {"small": small, "large": large, "all": small + large}[which]
        base = len(small) if which == "large" else 0
        return [pltpu.make_async_copy(a, b, sems.at[base + i]) for i, (a, b) in enumerate(pairs)]

    behind = [lax.rem(segment - section + 4, 4) for section in range(total_sections)]

    def each(section, act, which="all"):
        for j in range(4):

            @pl.when(behind[section] == j)
            def _(j=j):
                for copy in copies(section, j, which):
                    act(copy)

    def each_noise(act):
        for j in range(4):

            @pl.when(behind[total_sections - 1] == j)
            def _(j=j):
                for i in range(2):
                    source = noise_row(
                        j, i, cols, r["noise"].at[segment], r["got1_1"], r["noise_far"], r["got3_0"]
                    )
                    act(pltpu.make_async_copy(source, r["noise3"].at[i], r["strip_sems"].at[4, i]))

    def start(copy):
        copy.start()

    def wait(copy):
        copy.wait()

    strip_keys = list(moves)
    for copy in moves[strip_keys[0]]:
        copy.start()
    each(sections[0], start)

    def sigma(section):
        moment = r["times"][segment, section, STEPS - 1].astype(jnp.float32)
        return jnp.full((1, channels), moment, jnp.float32) / 1000.0

    pooled = jnp.sum(r["parts"][...], axis=0)
    place = lax.broadcasted_iota(jnp.int32, (cols, channels), 0)
    for copy in moves["xs" if leading else "noise0"]:
        copy.wait()
    if not leading:
        sigma0 = sigma(0)
        for i in range(xs.shape[0]):
            noisy = r["before"][i] + sigma0 * r["noise0"][i].astype(jnp.float32)
            xs[i] = noisy.astype(jnp.bfloat16)

    source = xs
    for section in sections:
        conv_now, film_now, gain_now = weights_of(section)
        each(section, wait, "small")
        gains = gain_now[...].astype(jnp.float32)
        gain = gains[0:1] + gains[1:2] + gains[2:3]
        gain = jnp.where(behind[section] == 0, r["gain"][...], gain)
        noise_scale = sigma(section)
        for step in range(STEPS):
            left_over = (total_sections - section) * STEPS - step
            count = own + 2 * left_over
            for i in range(count):
                values = source[i].astype(jnp.float32)
                inv = lax.rsqrt(jnp.mean(values * values, axis=-1, keepdims=True) + 1e-06)
                normed = values * inv * gain
                if i < left_over or i >= left_over + own:
                    image_row = row * own - left_over + i
                    inside = (image_row >= 0) & (image_row < height)
                    normed = jnp.where(inside, normed, 0.0)
                at = pl.ds(i * cols, cols)
                left = jnp.where(place == 0, 0.0, pltpu.roll(normed, 1, 0))
                right = jnp.where(place == cols - 1, 0.0, pltpu.roll(normed, cols - 1, 0))
                lhs[at, 0:channels] = left.astype(jnp.bfloat16)
                lhs[at, channels : 2 * channels] = normed.astype(jnp.bfloat16)
                lhs[at, 2 * channels :] = right.astype(jnp.bfloat16)
            if step == 0:
                cond = pooled + r["tpart"][STEPS * section : STEPS * (section + 1)]
                cond = cond.astype(jnp.bfloat16)
                scales = 1.0 + jnp.dot(cond, film_now[0], preferred_element_type=jnp.float32)
                shifts = jnp.dot(cond, film_now[1], preferred_element_type=jnp.float32)
                each(section, wait, "large")
                if section == sections[0]:
                    for later in sections[1:]:
                        each(later, start)
                    for key in strip_keys[1:]:
                        for copy in moves[key]:
                            copy.start()
                    if not leading:
                        each_noise(start)
            last = step == STEPS - 1
            noised = last and section > 0
            if noised and section < total_sections - 1:
                for copy in moves["noise%d" % section]:
                    copy.wait()
            elif noised:
                each_noise(wait)
            if not last:
                target = mid
            elif section == sections[-1]:
                target = r["out"]
            else:
                target = xs
            for i in range(count - 2):
                window = jnp.concatenate(
                    [lhs[pl.ds((i + dy) * cols, cols), :] for dy in range(3)], axis=1
                )
                total = jnp.dot(window, conv_now[...], preferred_element_type=jnp.float32)
                moved = total * scales[step : step + 1] + shifts[step : step + 1]
                branch = moved * (0.5 + 0.5 * jnp.tanh(0.5 * moved))
                after = source[i + 1].astype(jnp.float32) + branch
                if noised:
                    fresh = r["noise%d" % section][i].astype(jnp.float32)
                    after = after + noise_scale * fresh
                target[i] = after.astype(target.dtype)
            source = target


def cascade(group, operands, out_dtype, taps, channels, cols, own, sections, height):
    rows = own + 2 * STEPS * (sections - group[0])
    out_rows = own + 2 * STEPS * (sections - 1 - group[-1])
    outputs = {"out": jax.ShapeDtypeStruct((out_rows, cols, channels), out_dtype)}
    scratch = {
        "xs": pltpu.VMEM((rows, cols, channels), jnp.bfloat16),
        "mid": pltpu.VMEM((rows, cols, channels), jnp.bfloat16),
        "lhs": pltpu.VMEM((rows * cols, 3 * channels), jnp.bfloat16),
        "sems": pltpu.SemaphoreType.DMA((sections, 7)),
        "strip_sems": pltpu.SemaphoreType.DMA((5, 9)),
    }
    slots = len(group)
    scratch["conv_buf"] = pltpu.VMEM((slots, taps, channels), jnp.bfloat16)
    scratch["film_buf"] = pltpu.VMEM((slots, 2, channels, channels), jnp.bfloat16)
    scratch["gain_buf"] = pltpu.VMEM((slots, GAIN_ROWS, channels), jnp.bfloat16)
    if group[0] > 0:
        for section in range(sections):
            noise_rows = own + 2 * STEPS * (sections - 1 - section)
            scratch["noise%d" % section] = pltpu.VMEM((noise_rows, cols, channels), jnp.bfloat16)
    names = tuple(operands) + tuple(outputs) + tuple(scratch)
    steps = [own + 2 * STEPS * (sections - s) - 2 * (k + 1) for s in group for k in range(STEPS)]
    flops = 2 * sum(steps) * cols * taps * channels
    return pl.pallas_call(
        functools.partial(cascade_kernel, group, height, names),
        out_shape=list(outputs.values()),
        in_specs=[spec for _, spec in operands.values()],
        out_specs=[pl.BlockSpec(memory_space=pltpu.VMEM)] * len(outputs),
        scratch_shapes=list(scratch.values()),
        cost_estimate=pl.CostEstimate(
            flops=2 * flops, bytes_accessed=2 * sections * taps * channels, transcendentals=0
        ),
        compiler_params=pltpu.CompilerParams(vmem_limit_bytes=24 * MIB),
    )(*[value for value, _ in operands.values()])


def body(
    latents, noise, timesteps, text, text_weight, time_weight, film_weight, conv_weight, norm_gain
):
    sections = lax.axis_size("segment")
    count = lax.axis_size("row")
    own, cols, channels = latents.shape[1:]
    height = own * count
    taps = 9 * channels
    half = taps // 2

    vmem = pl.BlockSpec(memory_space=pltpu.VMEM)
    smem = pl.BlockSpec(memory_space=pltpu.SMEM)
    hbm = pl.BlockSpec(memory_space=pltpu.HBM)

    swap_cores = [(i, i ^ 1) for i in range(count)]
    chips = {d: [(i, (i + (2 * d, -2 * d)[i % 2]) % count) for i in range(count)] for d in (1, 2)}

    def turned(value, k):
        return lax.ppermute(value, "segment", [(i, (i + k) % sections) for i in range(sections)])

    conv = conv_weight.reshape(taps, channels)
    film = film_weight[0]
    strip = jax.ShapeDtypeStruct((own, cols, channels), jnp.bfloat16)
    cut = (half + channels) // 2 // 16 * 16
    pay_shapes = [
        jax.ShapeDtypeStruct((rows, channels), jnp.bfloat16)
        for rows in (cut, half - cut + channels + GAIN_ROWS)
    ]
    more_shapes = [
        jax.ShapeDtypeStruct((value.shape[0] + own * cols, channels), jnp.bfloat16)
        for value in pay_shapes
    ]
    x, pay0, pay1, more0, more1, noise_far = pl.pallas_call(
        prepare_kernel,
        out_shape=[strip, *pay_shapes, *more_shapes, strip],
        in_specs=[hbm] * 4 + [vmem],
        out_specs=[vmem] * 6,
        scratch_shapes=[pltpu.SemaphoreType.DMA((12,))],
        compiler_params=pltpu.CompilerParams(vmem_limit_bytes=57 * MIB),
    )(latents, noise[0], conv, film, norm_gain)
    got = {1: [turned(pay0, 1), None], 3: [None, turned(pay1, 3)]}
    got[1][1] = turned(more1, 1)
    got[3][0] = turned(more0, 3)
    noise_far = turned(noise_far, 2)
    x_core = lax.ppermute(x, "row", swap_cores)
    both = jnp.concatenate([x, x_core])
    near = lax.ppermute(both, "row", chips[1])
    far = lax.ppermute(both, "row", chips[2])
    back = lax.ppermute(jnp.concatenate([near, far[own:]]), "row", swap_cores)

    parts, tpart = pl.pallas_call(
        condition_kernel,
        out_shape=[
            jax.ShapeDtypeStruct((count, 1, channels), jnp.float32),
            jax.ShapeDtypeStruct((sections * STEPS, channels), jnp.float32),
        ],
        in_specs=[smem, vmem, vmem, vmem, hbm],
        out_specs=[vmem, vmem],
        compiler_params=pltpu.CompilerParams(vmem_limit_bytes=4 * MIB),
    )(timesteps, text, text_weight, time_weight, x_core)
    parts = lax.all_to_all(parts, "row", split_axis=0, concat_axis=0, tiled=True)

    firsts = (got[1][0], got[3][1])
    got[1][0], got[3][1] = pl.pallas_call(
        after_kernel,
        out_shape=[jax.ShapeDtypeStruct(v.shape, v.dtype) for v in firsts],
        in_specs=[hbm] * 3,
        out_specs=[hbm] * 2,
        input_output_aliases={0: 0, 1: 1},
        compiler_params=pltpu.CompilerParams(vmem_limit_bytes=MIB),
    )(*firsts, parts)
    got[2] = [turned(got[1][0], 1), turned(got[3][1], 3)]

    n = pl.pallas_call(
        choose_kernel,
        out_shape=jax.ShapeDtypeStruct((3 * own, cols, channels), jnp.bfloat16),
        in_specs=[hbm] * 5,
        out_specs=vmem,
        scratch_shapes=[pltpu.SemaphoreType.DMA((3, 2))],
        compiler_params=pltpu.CompilerParams(vmem_limit_bytes=4 * MIB),
    )(noise[0], got[1][1], noise_far, got[3][0], got[1][0])
    n_core = lax.ppermute(n, "row", swap_cores)
    n_near = lax.ppermute(jnp.concatenate([n[: 2 * own], n_core]), "row", chips[1])
    n_far = lax.ppermute(n_core[:own], "row", chips[2])
    n_back = lax.ppermute(
        jnp.concatenate([n_near[:own], n_near[2 * own : 4 * own]]), "row", swap_cores
    )
    swap = {k: [lax.ppermute(value, "row", swap_cores) for value in got[k]] for k in (1, 3, 2)}

    shared = {
        "times": (timesteps, smem),
        "parts": (parts, vmem),
        "tpart": (tpart, vmem),
        "gain": (norm_gain, vmem),
        "conv": (conv, hbm),
        "film": (film, hbm),
    }
    for k in (1, 2, 3):
        for i in range(2):
            shared["got%d_%d" % (k, i)] = (got[k][i], hbm)
            shared["swap%d_%d" % (k, i)] = (swap[k][i], hbm)
    values = {"latents": latents, "x_core": x_core, "near": near, "far": far, "back": back}
    first = dict(shared, **{key: (value, hbm) for key, value in values.items()})
    shape = (taps, channels, cols, own, sections, height)
    (before,) = cascade((0,), first, jnp.float32, *shape)
    values = {"n": n, "n_core": n_core, "n_near": n_near, "n_far": n_far, "n_back": n_back}
    values.update({"noise": noise[0], "noise_far": noise_far})
    second = dict(shared, **{key: (value, hbm) for key, value in values.items()})
    second["before"] = (before, vmem)
    (x,) = cascade(tuple(range(1, sections)), second, jnp.bfloat16, *shape)
    return x[None]


def solution(mesh):
    in_specs = (
        P(None, "row", None, None),
        P("segment", None, "row", None, None),
        P(),
        P("segment", None, "row"),
        P("row", None),
        P(),
        P("segment", None, None),
        P("segment", None, None, None, None),
        P("segment", None),
    )
    out_specs = P("segment", "row", None, None)
    return jax.shard_map(body, mesh=mesh, in_specs=in_specs, out_specs=out_specs, check_vma=False)
```

```python
import functools
import math

import jax
import jax.numpy as jnp
from jax import lax
from jax.experimental import pallas as pl
from jax.experimental.pallas import tpu as pltpu
from jax.sharding import PartitionSpec as P

STEPS = 2
GAIN_ROWS = 16
MIB = 1024 * 1024


def place_of_device():
    row = lax.axis_index("row")
    return lax.axis_index("segment"), row, lax.rem(row, 2)


def prepare_kernel(latents, noise, conv, film, gain, x_out, pay1, pay2, pay3, sems):
    segment, _, core = place_of_device()
    half = conv.shape[0] // 2
    channels = conv.shape[1]
    cols = latents.shape[2]
    pays = (pay1, pay2, pay3)
    here = pl.ds(pl.multiple_of(core * half, half), half)
    pairs = [(latents.at[segment], x_out)]
    for k, target in enumerate(pays):
        pairs.append((conv.at[here], target.at[pl.ds(0, half)]))
        for i in range(2):
            source = noise.at[lax.rem(segment + k + 1, 4), i]
            at = half + channels + GAIN_ROWS + i * cols
            pairs.append((source, target.at[pl.ds(at, cols)]))
    copies = [pltpu.make_async_copy(a, b, sems.at[i]) for i, (a, b) in enumerate(pairs)]
    film_at = pl.ds(half, channels)
    sides = [
        [
            pltpu.make_async_copy(
                film.at[:, i * channels : (i + 1) * channels], target.at[film_at], sems.at[10 + j]
            )
            for j, target in enumerate(pays)
        ]
        for i in range(2)
    ]
    for copy in copies:
        copy.start()
    for i in range(2):

        @pl.when(core == i)
        def _(i=i):
            for copy in sides[i]:
                copy.start()

    exact = gain[...]
    top = exact.astype(jnp.bfloat16).astype(jnp.float32)
    middle = (exact - top).astype(jnp.bfloat16).astype(jnp.float32)
    low = exact - top - middle
    line = lax.broadcasted_iota(jnp.int32, (GAIN_ROWS, channels), 0)
    rows = jnp.where(line == 0, top, jnp.where(line == 1, middle, jnp.where(line == 2, low, 0.0)))
    for target in pays:
        target[pl.ds(half + channels, GAIN_ROWS), :] = rows.astype(jnp.bfloat16)
    for copy in copies:
        copy.wait()
    for i in range(2):

        @pl.when(core == i)
        def _(i=i):
            for copy in sides[i]:
                copy.wait()


def condition_kernel(times, text, text_weight, time_weight, back, parts_out, tpart_out):
    segment, _, _ = place_of_device()
    tokens = text.shape[1]
    channels = time_weight.shape[0]
    total = jnp.sum(text[0].astype(jnp.float32), axis=0, keepdims=True)
    mean = (total / tokens).astype(jnp.bfloat16)
    part = jnp.dot(mean, text_weight[...], preferred_element_type=jnp.float32)
    parts_out[...] = jnp.broadcast_to(part[None], parts_out.shape)
    count = tpart_out.shape[0]
    half = channels // 2
    line = lax.broadcasted_iota(jnp.int32, (count, half), 0)
    moments = jnp.zeros((count, half), jnp.float32)
    for i in range(count):
        now = times[segment, i // STEPS, i % STEPS].astype(jnp.float32)
        moments = jnp.where(line == i, now, moments)
    place = lax.broadcasted_iota(jnp.int32, (count, half), 1).astype(jnp.float32)
    angles = moments * jnp.exp(-math.log(10000.0) * place / half)
    embed = jnp.concatenate([jnp.cos(angles), jnp.sin(angles)], axis=-1).astype(jnp.bfloat16)
    value = jnp.dot(embed, time_weight[...], preferred_element_type=jnp.float32)
    tpart_out[...] = value * (0.5 + 0.5 * jnp.tanh(0.5 * value))


def choose_kernel(noise, got1, got2, got3, parts, n_out, sems):
    segment, _, _ = place_of_device()
    sections = 4
    cols = n_out.shape[1]
    for act in ("start", "wait"):
        for section in range(sections - 1):
            behind = lax.rem(segment - section + sections, sections)
            for j in range(sections):

                @pl.when(behind == j)
                def _(j=j, section=section):
                    for i in range(2):
                        source = noise_row(j, i, cols, noise.at[segment], got1, got2, got3)
                        target = n_out.at[2 * section + i]
                        copy = pltpu.make_async_copy(source, target, sems.at[section, i])
                        getattr(copy, act)()


def noise_row(j, i, cols, own, *got):
    if j == 0:
        return own.at[i]
    source = got[j - 1]
    return source.at[pl.ds(source.shape[0] - (2 - i) * cols, cols)]


def return_kernel(near, far, before, out):
    out[0:2] = near[0:2]
    out[2:6] = near[4:8]


def cascade_kernel(sections, height, names, *refs):
    r = dict(zip(names, refs))
    segment, row, core = place_of_device()
    conv_buf, film_buf, gain_buf, sems = (r["conv_buf"], r["film_buf"], r["gain_buf"], r["sems"])
    lhs, mid, xs = r["lhs"], r["mid"], r["xs"]
    taps, channels = conv_buf.shape[1:]
    cols = xs.shape[1]
    half = taps // 2
    own = 2
    total_sections = r["tpart"].shape[0] // STEPS
    behind = [lax.rem(segment - section + 4, 4) for section in sections]


    def copies(slot, j):
        weights, films, gains = conv_buf.at[slot], film_buf.at[slot], gain_buf.at[slot]
        if j == 0:
            pairs = [
                (r["conv"], weights),
                (r["film"].at[:, :channels], films.at[0]),
                (r["film"].at[:, channels:], films.at[1]),
            ]
        else:
            pairs = []
            for key, side in (("got", core), ("swap", 1 - core)):
                source = r["%s%d" % (key, j)]
                at = pl.multiple_of(side * half, half)
                pairs.append((source.at[pl.ds(0, half)], weights.at[pl.ds(at, half)]))
                pairs.append((source.at[pl.ds(half, channels)], films.at[side]))
            pairs.append((r["got%d" % j].at[pl.ds(half + channels, GAIN_ROWS)], gains))
        if sections[slot] == total_sections - 1:
            for i in range(2):
                got = (r["got%d" % k] for k in (1, 2, 3))
                source = noise_row(j, i, cols, r["noise"].at[segment], *got)
                pairs.append((source, r["noise3"].at[i]))
        return [pltpu.make_async_copy(a, b, sems.at[slot, i]) for i, (a, b) in enumerate(pairs)]

    def each(slot, act):
        for j in range(4):

            @pl.when(behind[slot] == j)
            def _(j=j):
                for copy in copies(slot, j):
                    act(copy)

    strips = {}
    if sections[0] == 0:
        near, far, back = (r["near"], r["far"], r["back"])
        strips["xs"] = [
            (r["latents"].at[segment], 8, 8),
            (r["x_core"], 10, 6),
            (near.at[0:2], 4, 12),
            (near.at[2:4], 6, 10),
            (far.at[0:2], 0, 16),
            (far.at[2:4], 2, 14),
            (back.at[0:2], 14, 2),
            (back.at[2:4], 12, 4),
            (back.at[4:6], 16, 0),
        ]
    else:
        (n, n_core, n_near, n_far, n_back) = (
            r[key] for key in ("n", "n_core", "n_near", "n_far", "n_back")
        )
        strips["noise0"] = [
            (n.at[0:2], 6, 6),
            (n_core.at[0:2], 8, 4),
            (n_near.at[0:2], 2, 10),
            (n_near.at[4:6], 4, 8),
            (n_far, 0, 12),
            (n_back.at[0:2], 12, 0),
            (n_back.at[2:4], 10, 2),
        ]
        strips["noise1"] = [
            (n.at[2:4], 4, 4),
            (n_core.at[2:4], 6, 2),
            (n_near.at[2:4], 0, 8),
            (n_near.at[6:8], 2, 6),
            (n_back.at[4:6], 8, 0),
        ]
        strips["noise2"] = [(n.at[4:6], 2, 2), (n_core.at[4:6], 4, 0), (n_near.at[8:10], 0, 4)]
    moves = {}
    for key, placed in strips.items():
        moves[key] = []
        for i, (value, first, second) in enumerate(placed):
            target = r[key].at[pl.ds(first + core * (second - first), 2)]
            moves[key].append(pltpu.make_async_copy(value, target, r["strip_sems"].at[len(moves), i]))

    first = next(iter(strips))
    for copy in moves[first]:
        copy.start()
    for slot in range(len(sections)):
        each(slot, lambda copy: copy.start())
    for key in moves:
        if key != first:
            for copy in moves[key]:
                copy.start()
    for copy in moves[first]:
        copy.wait()

    def sigma(section):
        moment = r["times"][segment, section, STEPS - 1].astype(jnp.float32)
        return jnp.full((1, channels), moment, jnp.float32) / 1000.0

    source = xs
    if sections[0] > 0:
        sigma0 = sigma(0)
        for i in range(xs.shape[0]):
            noisy = r["before"][i] + sigma0 * r["noise0"][i].astype(jnp.float32)
            xs[i] = noisy.astype(jnp.bfloat16)

    pooled = jnp.sum(r["parts"][...], axis=0)
    place = lax.broadcasted_iota(jnp.int32, (cols, channels), 0)
    for slot, section in enumerate(sections):
        each(slot, lambda copy: copy.wait())
        gains = gain_buf[slot].astype(jnp.float32)
        gain = gains[0:1] + gains[1:2] + gains[2:3]
        gain = jnp.where(behind[slot] == 0, r["gain"][...], gain)
        cond = (pooled + r["tpart"][STEPS * section : STEPS * (section + 1)]).astype(jnp.bfloat16)
        scales = 1.0 + jnp.dot(cond, film_buf[slot, 0], preferred_element_type=jnp.float32)
        shifts = jnp.dot(cond, film_buf[slot, 1], preferred_element_type=jnp.float32)
        for step in range(STEPS):
            left_over = (total_sections - section) * STEPS - step
            count = own + 2 * left_over
            for i in range(count):
                values = source[i].astype(jnp.float32)
                inv = lax.rsqrt(jnp.mean(values * values, axis=-1, keepdims=True) + 1e-06)
                normed = values * inv * gain
                if i < left_over or i >= left_over + own:
                    image_row = row * own - left_over + i
                    inside = (image_row >= 0) & (image_row < height)
                    normed = jnp.where(inside, normed, 0.0)
                at = pl.ds(i * cols, cols)
                left = jnp.where(place == 0, 0.0, pltpu.roll(normed, 1, 0))
                right = jnp.where(place == cols - 1, 0.0, pltpu.roll(normed, cols - 1, 0))
                lhs[at, 0:channels] = left.astype(jnp.bfloat16)
                lhs[at, channels : 2 * channels] = normed.astype(jnp.bfloat16)
                lhs[at, 2 * channels :] = right.astype(jnp.bfloat16)
            last = step == STEPS - 1
            noised = last and section > 0
            if noised and section < total_sections - 1:
                for copy in moves["noise%d" % section]:
                    copy.wait()
            if not last:
                target = mid
            elif slot == len(sections) - 1:
                target = r["out"]
            else:
                target = xs
            for i in range(count - 2):
                window = jnp.concatenate(
                    [lhs[pl.ds((i + dy) * cols, cols), :] for dy in range(3)], axis=1
                )
                total = jnp.dot(window, conv_buf[slot], preferred_element_type=jnp.float32)
                moved = total * scales[step : step + 1] + shifts[step : step + 1]
                branch = moved * (0.5 + 0.5 * jnp.tanh(0.5 * moved))
                after = source[i + 1].astype(jnp.float32) + branch
                if noised:
                    fresh = r["noise%d" % section][i].astype(jnp.float32)
                    after = after + sigma(section) * fresh
                target[i] = after.astype(target.dtype)
            source = target


def cascade(group, operands, dtype, taps, channels, cols, own, sections, height):
    slots = len(group)
    rows = own + 2 * STEPS * (sections - group[0])
    out_rows = own + 2 * STEPS * (sections - 1 - group[-1])
    scratch = {
        "conv_buf": pltpu.VMEM((slots, taps, channels), jnp.bfloat16),
        "film_buf": pltpu.VMEM((slots, 2, channels, channels), jnp.bfloat16),
        "gain_buf": pltpu.VMEM((slots, GAIN_ROWS, channels), jnp.bfloat16),
        "xs": pltpu.VMEM((rows, cols, channels), jnp.bfloat16),
        "mid": pltpu.VMEM((rows, cols, channels), jnp.bfloat16),
        "lhs": pltpu.VMEM((rows * cols, 3 * channels), jnp.bfloat16),
        "sems": pltpu.SemaphoreType.DMA((slots, 9)),
        "strip_sems": pltpu.SemaphoreType.DMA((4, 9)),
    }
    if group[0] > 0:
        for section in range(sections):
            noise_rows = own + 2 * STEPS * (sections - 1 - section)
            scratch["noise%d" % section] = pltpu.VMEM((noise_rows, cols, channels), jnp.bfloat16)
    names = tuple(operands) + ("out",) + tuple(scratch)
    steps = [own + 2 * STEPS * (sections - s) - 2 * (k + 1) for s in group for k in range(STEPS)]
    flops = 2 * sum(steps) * cols * taps * channels
    return pl.pallas_call(
        functools.partial(cascade_kernel, group, height, names),
        out_shape=jax.ShapeDtypeStruct((out_rows, cols, channels), dtype),
        in_specs=[spec for _, spec in operands.values()],
        out_specs=pl.BlockSpec(memory_space=pltpu.VMEM),
        scratch_shapes=list(scratch.values()),
        cost_estimate=pl.CostEstimate(
            flops=flops, bytes_accessed=2 * slots * taps * channels, transcendentals=0
        ),
        compiler_params=pltpu.CompilerParams(vmem_limit_bytes=24 * MIB),
    )(*[value for value, _ in operands.values()])


def body(
    latents, noise, timesteps, text, text_weight, time_weight, film_weight, conv_weight, norm_gain
):
    sections = lax.axis_size("segment")
    count = lax.axis_size("row")
    own, cols, channels = latents.shape[1:]
    height = own * count
    taps = 9 * channels
    half = taps // 2

    vmem = pl.BlockSpec(memory_space=pltpu.VMEM)
    smem = pl.BlockSpec(memory_space=pltpu.SMEM)
    hbm = pl.BlockSpec(memory_space=pltpu.HBM)

    swap_cores = [(i, i ^ 1) for i in range(count)]
    chips = {d: [(i, (i + (2 * d, -2 * d)[i % 2]) % count) for i in range(count)] for d in (1, 2)}

    def turned(value, k):
        return lax.ppermute(value, "segment", [(i, (i + k) % sections) for i in range(sections)])

    conv = conv_weight.reshape(taps, channels)
    film = film_weight[0]
    strip = jax.ShapeDtypeStruct((own, cols, channels), jnp.bfloat16)
    pay_rows = half + channels + GAIN_ROWS + own * cols
    pay_shape = jax.ShapeDtypeStruct((pay_rows, channels), jnp.bfloat16)
    x, *pays = pl.pallas_call(
        prepare_kernel,
        out_shape=[strip, pay_shape, pay_shape, pay_shape],
        in_specs=[hbm] * 4 + [vmem],
        out_specs=[vmem] * 4,
        scratch_shapes=[pltpu.SemaphoreType.DMA((13,))],
        compiler_params=pltpu.CompilerParams(vmem_limit_bytes=57 * MIB),
    )(latents, noise[0], conv, film, norm_gain)
    got = {k: turned(pays[k - 1], k) for k in (1, 3, 2)}

    x_core = lax.ppermute(x, "row", swap_cores)
    both = jnp.concatenate([x, x_core])
    near = lax.ppermute(both, "row", chips[1])
    far = lax.ppermute(both, "row", chips[2])
    back = lax.ppermute(jnp.concatenate([near, far[own:]]), "row", swap_cores)

    parts, tpart = pl.pallas_call(
        condition_kernel,
        out_shape=[
            jax.ShapeDtypeStruct((count, 1, channels), jnp.float32),
            jax.ShapeDtypeStruct((sections * STEPS, channels), jnp.float32),
        ],
        in_specs=[smem, vmem, vmem, vmem, hbm],
        out_specs=[vmem, vmem],
        compiler_params=pltpu.CompilerParams(vmem_limit_bytes=4 * MIB),
    )(timesteps, text, text_weight, time_weight, back)
    parts = lax.all_to_all(parts, "row", split_axis=0, concat_axis=0, tiled=True)

    n = pl.pallas_call(
        choose_kernel,
        out_shape=jax.ShapeDtypeStruct((3 * own, cols, channels), jnp.bfloat16),
        in_specs=[hbm] * 5,
        out_specs=vmem,
        scratch_shapes=[pltpu.SemaphoreType.DMA((3, 2))],
        compiler_params=pltpu.CompilerParams(vmem_limit_bytes=4 * MIB),
    )(noise[0], got[1], got[2], got[3], parts)
    n_core = lax.ppermute(n, "row", swap_cores)
    n_near = lax.ppermute(jnp.concatenate([n[: 2 * own], n_core]), "row", chips[1])
    n_far = lax.ppermute(n_core[:own], "row", chips[2])
    swap = {k: lax.ppermute(got[k], "row", swap_cores) for k in (1, 3, 2)}

    shared = {
        "times": (timesteps, smem),
        "parts": (parts, vmem),
        "tpart": (tpart, vmem),
        "gain": (norm_gain, vmem),
        "conv": (conv, hbm),
        "film": (film, hbm),
    }
    for k in (1, 2, 3):
        shared["got%d" % k] = (got[k], hbm)
        shared["swap%d" % k] = (swap[k], hbm)
    values = {"latents": latents, "x_core": x_core, "near": near, "far": far, "back": back}
    first = dict(shared, **{key: (value, hbm) for key, value in values.items()})
    before = cascade((0,), first, jnp.float32, taps, channels, cols, own, sections, height)
    n_some = pl.pallas_call(
        return_kernel,
        out_shape=jax.ShapeDtypeStruct((3 * own, cols, channels), jnp.bfloat16),
        in_specs=[vmem, hbm, hbm],
        out_specs=vmem,
        compiler_params=pltpu.CompilerParams(vmem_limit_bytes=4 * MIB),
    )(n_near, n_far, before)
    n_back = lax.ppermute(n_some, "row", swap_cores)
    values = {"n": n, "n_core": n_core, "n_near": n_near, "n_far": n_far, "n_back": n_back}
    values.update({"noise": noise[0]})
    second = dict(shared, **{key: (value, hbm) for key, value in values.items()})
    second["before"] = (before, vmem)
    later = tuple(range(1, sections))
    x = cascade(later, second, jnp.bfloat16, taps, channels, cols, own, sections, height)
    return x[None]


def solution(mesh):
    in_specs = (
        P(None, "row", None, None),
        P("segment", None, "row", None, None),
        P(),
        P("segment", None, "row"),
        P("row", None),
        P(),
        P("segment", None, None),
        P("segment", None, None, None, None),
        P("segment", None),
    )
    out_specs = P("segment", "row", None, None)
    return jax.shard_map(body, mesh=mesh, in_specs=in_specs, out_specs=out_specs, check_vma=False)
```

```python
import functools
import math

import jax
import jax.numpy as jnp
from jax import lax
from jax.experimental import pallas as pl
from jax.experimental.pallas import tpu as pltpu
from jax.sharding import PartitionSpec as P

STEPS = 2
GAIN_ROWS = 16
MIB = 1024 * 1024


def place_of_device():
    row = lax.axis_index("row")
    return lax.axis_index("segment"), row, lax.rem(row, 2)


def prepare_kernel(latents, noise, conv, film, gain, x_out, pay1, pay2, pay3, sems):
    segment, _, core = place_of_device()
    half = conv.shape[0] // 2
    channels = conv.shape[1]
    cols = latents.shape[2]
    pays = (pay1, pay2, pay3)
    here = pl.ds(pl.multiple_of(core * half, half), half)
    pairs = [(latents.at[segment], x_out)]
    for k, target in enumerate(pays):
        pairs.append((conv.at[here], target.at[pl.ds(0, half)]))
        for i in range(2):
            source = noise.at[lax.rem(segment + k + 1, 4), i]
            at = half + channels + GAIN_ROWS + i * cols
            pairs.append((source, target.at[pl.ds(at, cols)]))
    copies = [pltpu.make_async_copy(a, b, sems.at[i]) for i, (a, b) in enumerate(pairs)]
    film_at = pl.ds(half, channels)
    sides = [
        [
            pltpu.make_async_copy(
                film.at[:, i * channels : (i + 1) * channels], target.at[film_at], sems.at[10 + j]
            )
            for j, target in enumerate(pays)
        ]
        for i in range(2)
    ]
    for copy in copies:
        copy.start()
    for i in range(2):

        @pl.when(core == i)
        def _(i=i):
            for copy in sides[i]:
                copy.start()

    exact = gain[...]
    top = exact.astype(jnp.bfloat16).astype(jnp.float32)
    middle = (exact - top).astype(jnp.bfloat16).astype(jnp.float32)
    low = exact - top - middle
    line = lax.broadcasted_iota(jnp.int32, (GAIN_ROWS, channels), 0)
    rows = jnp.where(line == 0, top, jnp.where(line == 1, middle, jnp.where(line == 2, low, 0.0)))
    for target in pays:
        target[pl.ds(half + channels, GAIN_ROWS), :] = rows.astype(jnp.bfloat16)
    for copy in copies:
        copy.wait()
    for i in range(2):

        @pl.when(core == i)
        def _(i=i):
            for copy in sides[i]:
                copy.wait()


def condition_kernel(times, text, text_weight, time_weight, near, far, parts_out, tpart_out):
    segment, _, _ = place_of_device()
    tokens = text.shape[1]
    channels = time_weight.shape[0]
    total = jnp.sum(text[0].astype(jnp.float32), axis=0, keepdims=True)
    mean = (total / tokens).astype(jnp.bfloat16)
    part = jnp.dot(mean, text_weight[...], preferred_element_type=jnp.float32)
    parts_out[...] = jnp.broadcast_to(part[None], parts_out.shape)
    count = tpart_out.shape[0]
    half = channels // 2
    line = lax.broadcasted_iota(jnp.int32, (count, half), 0)
    moments = jnp.zeros((count, half), jnp.float32)
    for i in range(count):
        now = times[segment, i // STEPS, i % STEPS].astype(jnp.float32)
        moments = jnp.where(line == i, now, moments)
    place = lax.broadcasted_iota(jnp.int32, (count, half), 1).astype(jnp.float32)
    angles = moments * jnp.exp(-math.log(10000.0) * place / half)
    embed = jnp.concatenate([jnp.cos(angles), jnp.sin(angles)], axis=-1).astype(jnp.bfloat16)
    value = jnp.dot(embed, time_weight[...], preferred_element_type=jnp.float32)
    tpart_out[...] = value * (0.5 + 0.5 * jnp.tanh(0.5 * value))


def choose_kernel(noise, got1, got2, got3, parts, n_out, sems):
    segment, _, _ = place_of_device()
    sections = 4
    cols = n_out.shape[1]
    for act in ("start", "wait"):
        for section in range(sections - 1):
            behind = lax.rem(segment - section + sections, sections)
            for j in range(sections):

                @pl.when(behind == j)
                def _(j=j, section=section):
                    for i in range(2):
                        source = noise_row(j, i, cols, noise.at[segment], got1, got2, got3)
                        target = n_out.at[2 * section + i]
                        copy = pltpu.make_async_copy(source, target, sems.at[section, i])
                        getattr(copy, act)()


def noise_row(j, i, cols, own, *got):
    if j == 0:
        return own.at[i]
    source = got[j - 1]
    return source.at[pl.ds(source.shape[0] - (2 - i) * cols, cols)]


def return_kernel(near, far, before, out):
    out[0:2] = near[0:2]
    out[2:6] = near[4:8]


def cascade_kernel(sections, height, names, *refs):
    r = dict(zip(names, refs))
    segment, row, core = place_of_device()
    conv_buf, film_buf, gain_buf, sems = (r["conv_buf"], r["film_buf"], r["gain_buf"], r["sems"])
    lhs, mid, xs = r["lhs"], r["mid"], r["xs"]
    taps, channels = conv_buf.shape[1:]
    cols = xs.shape[1]
    half = taps // 2
    own = 2
    total_sections = r["tpart"].shape[0] // STEPS
    behind = [lax.rem(segment - section + 4, 4) for section in sections]


    def copies(slot, j):
        weights, films, gains = conv_buf.at[slot], film_buf.at[slot], gain_buf.at[slot]
        if j == 0:
            pairs = [
                (r["conv"], weights),
                (r["film"].at[:, :channels], films.at[0]),
                (r["film"].at[:, channels:], films.at[1]),
            ]
        else:
            pairs = []
            for key, side in (("got", core), ("swap", 1 - core)):
                source = r["%s%d" % (key, j)]
                at = pl.multiple_of(side * half, half)
                pairs.append((source.at[pl.ds(0, half)], weights.at[pl.ds(at, half)]))
                pairs.append((source.at[pl.ds(half, channels)], films.at[side]))
            pairs.append((r["got%d" % j].at[pl.ds(half + channels, GAIN_ROWS)], gains))
        if sections[slot] == total_sections - 1:
            for i in range(2):
                got = (r["got%d" % k] for k in (1, 2, 3))
                source = noise_row(j, i, cols, r["noise"].at[segment], *got)
                pairs.append((source, r["noise3"].at[i]))
        return [pltpu.make_async_copy(a, b, sems.at[slot, i]) for i, (a, b) in enumerate(pairs)]

    def each(slot, act):
        for j in range(4):

            @pl.when(behind[slot] == j)
            def _(j=j):
                for copy in copies(slot, j):
                    act(copy)

    strips = {}
    if sections[0] == 0:
        near, far, back = (r["near"], r["far"], r["back"])
        strips["xs"] = [
            (r["latents"].at[segment], 8, 8),
            (r["x_core"], 10, 6),
            (near.at[0:2], 4, 12),
            (near.at[2:4], 6, 10),
            (far.at[0:2], 0, 16),
            (far.at[2:4], 2, 14),
            (back.at[0:2], 14, 2),
            (back.at[2:4], 12, 4),
            (back.at[4:6], 16, 0),
        ]
    else:
        (n, n_core, n_near, n_far, n_back) = (
            r[key] for key in ("n", "n_core", "n_near", "n_far", "n_back")
        )
        strips["noise0"] = [
            (n.at[0:2], 6, 6),
            (n_core.at[0:2], 8, 4),
            (n_near.at[0:2], 2, 10),
            (n_near.at[4:6], 4, 8),
            (n_far, 0, 12),
            (n_back.at[0:2], 12, 0),
            (n_back.at[2:4], 10, 2),
        ]
        strips["noise1"] = [
            (n.at[2:4], 4, 4),
            (n_core.at[2:4], 6, 2),
            (n_near.at[2:4], 0, 8),
            (n_near.at[6:8], 2, 6),
            (n_back.at[4:6], 8, 0),
        ]
        strips["noise2"] = [(n.at[4:6], 2, 2), (n_core.at[4:6], 4, 0), (n_near.at[8:10], 0, 4)]
    moves = {}
    for key, placed in strips.items():
        moves[key] = []
        for i, (value, first, second) in enumerate(placed):
            target = r[key].at[pl.ds(first + core * (second - first), 2)]
            moves[key].append(pltpu.make_async_copy(value, target, r["strip_sems"].at[len(moves), i]))

    first = next(iter(strips))
    for copy in moves[first]:
        copy.start()
    for slot in range(len(sections)):
        each(slot, lambda copy: copy.start())
    for key in moves:
        if key != first:
            for copy in moves[key]:
                copy.start()
    for copy in moves[first]:
        copy.wait()

    def sigma(section):
        moment = r["times"][segment, section, STEPS - 1].astype(jnp.float32)
        return jnp.full((1, channels), moment, jnp.float32) / 1000.0

    source = xs
    if sections[0] > 0:
        sigma0 = sigma(0)
        for i in range(xs.shape[0]):
            noisy = r["before"][i] + sigma0 * r["noise0"][i].astype(jnp.float32)
            xs[i] = noisy.astype(jnp.bfloat16)

    pooled = jnp.sum(r["parts"][...], axis=0)
    place = lax.broadcasted_iota(jnp.int32, (cols, channels), 0)
    for slot, section in enumerate(sections):
        each(slot, lambda copy: copy.wait())
        gains = gain_buf[slot].astype(jnp.float32)
        gain = gains[0:1] + gains[1:2] + gains[2:3]
        gain = jnp.where(behind[slot] == 0, r["gain"][...], gain)
        cond = (pooled + r["tpart"][STEPS * section : STEPS * (section + 1)]).astype(jnp.bfloat16)
        scales = 1.0 + jnp.dot(cond, film_buf[slot, 0], preferred_element_type=jnp.float32)
        shifts = jnp.dot(cond, film_buf[slot, 1], preferred_element_type=jnp.float32)
        for step in range(STEPS):
            left_over = (total_sections - section) * STEPS - step
            count = own + 2 * left_over
            for i in range(count):
                values = source[i].astype(jnp.float32)
                inv = lax.rsqrt(jnp.mean(values * values, axis=-1, keepdims=True) + 1e-06)
                normed = values * inv * gain
                if i < left_over or i >= left_over + own:
                    image_row = row * own - left_over + i
                    inside = (image_row >= 0) & (image_row < height)
                    normed = jnp.where(inside, normed, 0.0)
                at = pl.ds(i * cols, cols)
                left = jnp.where(place == 0, 0.0, pltpu.roll(normed, 1, 0))
                right = jnp.where(place == cols - 1, 0.0, pltpu.roll(normed, cols - 1, 0))
                lhs[at, 0:channels] = left.astype(jnp.bfloat16)
                lhs[at, channels : 2 * channels] = normed.astype(jnp.bfloat16)
                lhs[at, 2 * channels :] = right.astype(jnp.bfloat16)
            last = step == STEPS - 1
            noised = last and section > 0
            if noised and section < total_sections - 1:
                for copy in moves["noise%d" % section]:
                    copy.wait()
            if not last:
                target = mid
            elif slot == len(sections) - 1:
                target = r["out"]
            else:
                target = xs
            for i in range(count - 2):
                window = jnp.concatenate(
                    [lhs[pl.ds((i + dy) * cols, cols), :] for dy in range(3)], axis=1
                )
                total = jnp.dot(window, conv_buf[slot], preferred_element_type=jnp.float32)
                moved = total * scales[step : step + 1] + shifts[step : step + 1]
                branch = moved * (0.5 + 0.5 * jnp.tanh(0.5 * moved))
                after = source[i + 1].astype(jnp.float32) + branch
                if noised:
                    fresh = r["noise%d" % section][i].astype(jnp.float32)
                    after = after + sigma(section) * fresh
                target[i] = after.astype(target.dtype)
            source = target


def cascade(group, operands, dtype, taps, channels, cols, own, sections, height):
    slots = len(group)
    rows = own + 2 * STEPS * (sections - group[0])
    out_rows = own + 2 * STEPS * (sections - 1 - group[-1])
    scratch = {
        "conv_buf": pltpu.VMEM((slots, taps, channels), jnp.bfloat16),
        "film_buf": pltpu.VMEM((slots, 2, channels, channels), jnp.bfloat16),
        "gain_buf": pltpu.VMEM((slots, GAIN_ROWS, channels), jnp.bfloat16),
        "xs": pltpu.VMEM((rows, cols, channels), jnp.bfloat16),
        "mid": pltpu.VMEM((rows, cols, channels), jnp.bfloat16),
        "lhs": pltpu.VMEM((rows * cols, 3 * channels), jnp.bfloat16),
        "sems": pltpu.SemaphoreType.DMA((slots, 9)),
        "strip_sems": pltpu.SemaphoreType.DMA((4, 9)),
    }
    if group[0] > 0:
        for section in range(sections):
            noise_rows = own + 2 * STEPS * (sections - 1 - section)
            scratch["noise%d" % section] = pltpu.VMEM((noise_rows, cols, channels), jnp.bfloat16)
    names = tuple(operands) + ("out",) + tuple(scratch)
    steps = [own + 2 * STEPS * (sections - s) - 2 * (k + 1) for s in group for k in range(STEPS)]
    flops = 2 * sum(steps) * cols * taps * channels
    return pl.pallas_call(
        functools.partial(cascade_kernel, group, height, names),
        out_shape=jax.ShapeDtypeStruct((out_rows, cols, channels), dtype),
        in_specs=[spec for _, spec in operands.values()],
        out_specs=pl.BlockSpec(memory_space=pltpu.VMEM),
        scratch_shapes=list(scratch.values()),
        cost_estimate=pl.CostEstimate(
            flops=flops, bytes_accessed=2 * slots * taps * channels, transcendentals=0
        ),
        compiler_params=pltpu.CompilerParams(vmem_limit_bytes=24 * MIB),
    )(*[value for value, _ in operands.values()])


def body(
    latents, noise, timesteps, text, text_weight, time_weight, film_weight, conv_weight, norm_gain
):
    sections = lax.axis_size("segment")
    count = lax.axis_size("row")
    own, cols, channels = latents.shape[1:]
    height = own * count
    taps = 9 * channels
    half = taps // 2

    vmem = pl.BlockSpec(memory_space=pltpu.VMEM)
    smem = pl.BlockSpec(memory_space=pltpu.SMEM)
    hbm = pl.BlockSpec(memory_space=pltpu.HBM)

    swap_cores = [(i, i ^ 1) for i in range(count)]
    chips = {d: [(i, (i + (2 * d, -2 * d)[i % 2]) % count) for i in range(count)] for d in (1, 2)}

    def turned(value, k):
        return lax.ppermute(value, "segment", [(i, (i + k) % sections) for i in range(sections)])

    conv = conv_weight.reshape(taps, channels)
    film = film_weight[0]
    strip = jax.ShapeDtypeStruct((own, cols, channels), jnp.bfloat16)
    pay_rows = half + channels + GAIN_ROWS + own * cols
    pay_shape = jax.ShapeDtypeStruct((pay_rows, channels), jnp.bfloat16)
    x, *pays = pl.pallas_call(
        prepare_kernel,
        out_shape=[strip, pay_shape, pay_shape, pay_shape],
        in_specs=[hbm] * 4 + [vmem],
        out_specs=[vmem] * 4,
        scratch_shapes=[pltpu.SemaphoreType.DMA((13,))],
        compiler_params=pltpu.CompilerParams(vmem_limit_bytes=57 * MIB),
    )(latents, noise[0], conv, film, norm_gain)
    got = {k: turned(pays[k - 1], k) for k in (1, 3, 2)}

    x_core = lax.ppermute(x, "row", swap_cores)
    both = jnp.concatenate([x, x_core])
    near = lax.ppermute(both, "row", chips[1])
    far = lax.ppermute(both, "row", chips[2])
    back = lax.ppermute(jnp.concatenate([near, far[own:]]), "row", swap_cores)

    parts, tpart = pl.pallas_call(
        condition_kernel,
        out_shape=[
            jax.ShapeDtypeStruct((count, 1, channels), jnp.float32),
            jax.ShapeDtypeStruct((sections * STEPS, channels), jnp.float32),
        ],
        in_specs=[smem, vmem, vmem, vmem, hbm, hbm],
        out_specs=[vmem, vmem],
        compiler_params=pltpu.CompilerParams(vmem_limit_bytes=4 * MIB),
    )(timesteps, text, text_weight, time_weight, near, far)
    parts = lax.all_to_all(parts, "row", split_axis=0, concat_axis=0, tiled=True)

    n = pl.pallas_call(
        choose_kernel,
        out_shape=jax.ShapeDtypeStruct((3 * own, cols, channels), jnp.bfloat16),
        in_specs=[hbm] * 5,
        out_specs=vmem,
        scratch_shapes=[pltpu.SemaphoreType.DMA((3, 2))],
        compiler_params=pltpu.CompilerParams(vmem_limit_bytes=4 * MIB),
    )(noise[0], got[1], got[2], got[3], parts)
    n_core = lax.ppermute(n, "row", swap_cores)
    n_near = lax.ppermute(jnp.concatenate([n[: 2 * own], n_core]), "row", chips[1])
    n_far = lax.ppermute(n_core[:own], "row", chips[2])
    swap = {k: lax.ppermute(got[k], "row", swap_cores) for k in (1, 3, 2)}

    shared = {
        "times": (timesteps, smem),
        "parts": (parts, vmem),
        "tpart": (tpart, vmem),
        "gain": (norm_gain, vmem),
        "conv": (conv, hbm),
        "film": (film, hbm),
    }
    for k in (1, 2, 3):
        shared["got%d" % k] = (got[k], hbm)
        shared["swap%d" % k] = (swap[k], hbm)
    values = {"latents": latents, "x_core": x_core, "near": near, "far": far, "back": back}
    first = dict(shared, **{key: (value, hbm) for key, value in values.items()})
    before = cascade((0,), first, jnp.float32, taps, channels, cols, own, sections, height)
    n_some = pl.pallas_call(
        return_kernel,
        out_shape=jax.ShapeDtypeStruct((3 * own, cols, channels), jnp.bfloat16),
        in_specs=[vmem, hbm, hbm],
        out_specs=vmem,
        compiler_params=pltpu.CompilerParams(vmem_limit_bytes=4 * MIB),
    )(n_near, n_far, before)
    n_back = lax.ppermute(n_some, "row", swap_cores)
    values = {"n": n, "n_core": n_core, "n_near": n_near, "n_far": n_far, "n_back": n_back}
    values.update({"noise": noise[0]})
    second = dict(shared, **{key: (value, hbm) for key, value in values.items()})
    second["before"] = (before, vmem)
    later = tuple(range(1, sections))
    x = cascade(later, second, jnp.bfloat16, taps, channels, cols, own, sections, height)
    return x[None]


def solution(mesh):
    in_specs = (
        P(None, "row", None, None),
        P("segment", None, "row", None, None),
        P(),
        P("segment", None, "row"),
        P("row", None),
        P(),
        P("segment", None, None),
        P("segment", None, None, None, None),
        P("segment", None),
    )
    out_specs = P("segment", "row", None, None)
    return jax.shard_map(body, mesh=mesh, in_specs=in_specs, out_specs=out_specs, check_vma=False)
```
